32 devices in a mesh: patch: 2 (over y), exp: 4 (over z), strip: 2 (over x), band: 2 (over core).
Axes of the slice: x: 2, y: 2, z: 4, core: 2. Of those that a mesh axis runs over, the one named last changes fastest.
Arguments:
- images: float32 [64, 64, 512], P(('patch', 'exp'), 'strip', 'band'), parts along dimension 0, may hold values from -80 to 80
- valid_mask: int32 [64, 64, 512], P(('patch', 'exp'), 'strip', 'band'), parts along dimension 0, may hold values from 0 to 1, as said below
- basis_index: int32 [64, 4, 2], P(('patch', 'exp'), 'strip'), parts along dimension 0, may hold values from 0 to 15
- match_index: int32 [64, 4, 2], P(('patch', 'exp'), 'strip'), parts along dimension 0, may hold values from 0 to 15
- psf_bank: float32 [16, 81], replicated, may hold values from 0.05 to 1
Outputs:
- coadd_image: float32 [128, 512], P(('patch', 'strip'), 'band'), parts along dimension 0
- difference: float32 [64, 64, 512], P(('patch', 'exp'), 'strip', 'band'), parts along dimension 0
The draws below stay inside these ranges and needn't reach their ends.
There are 2 independent parts, one for each index of `patch`. The reference program is written for one: setup_inputs(seed, part) draws one part's arguments, and reference() takes and returns one part's arrays. A program takes and returns all parts, laid end to end along the dimension named above; an argument that names none is the same for every part. Nothing has to cross between parts.
Inputs may be any that keep to these rules, and one draw needn't show every extreme that they name: `valid_mask`: one marks a valid pixel of that exposure.
All inputs are finite; a program needn't handle non-finite values.
Results may differ from the reference program's by a relative error of at most 0.0003.
Values sent between devices are 32-bit elements; how exact they have to be, the bound alone decides.
A program may use at most 128 MiB of HBM per device.

```python
import math
import jax
import jax.numpy as jnp
from jax import lax

TILE_ROWS = 16
KERNEL = 9
BASES = 16
EXPOSURES = 32
HEIGHT = 64
WIDTH = 512
TILES = 4


def stack_bits(key):
    shape_all = (EXPOSURES, HEIGHT, WIDTH)
    valid_bits = jax.random.randint(jax.random.fold_in(key, 101), shape_all, 0, 10)
    valid_mask = (valid_bits < 9).astype(jnp.int32)
    hit_bits = jax.random.randint(jax.random.fold_in(key, 102), shape_all, 0, 100)
    return (valid_mask, hit_bits)


def blob_field(key, salt_base, rate_permille):
    block_side = 16
    coarse_shape = (EXPOSURES, HEIGHT // block_side + 2, WIDTH // block_side + 2)
    hit_draw = jax.random.randint(jax.random.fold_in(key, salt_base), coarse_shape, 0, 1000)
    amplitude = 20.0 + 30.0 * jax.random.uniform(jax.random.fold_in(key, salt_base + 1), coarse_shape, jnp.float32)
    coarse_field = jnp.where(hit_draw < rate_permille, amplitude, 0.0)
    shift_rows = jax.random.randint(jax.random.fold_in(key, salt_base + 2), (EXPOSURES, 1, 1), 0, block_side)
    shift_cols = jax.random.randint(jax.random.fold_in(key, salt_base + 3), (EXPOSURES, 1, 1), 0, block_side)
    row_block = (jnp.arange(HEIGHT, dtype=jnp.int32)[None, :, None] + shift_rows) // block_side
    col_block = (jnp.arange(WIDTH, dtype=jnp.int32)[None, None, :] + shift_cols) // block_side
    exposure_ids = jnp.arange(EXPOSURES, dtype=jnp.int32)[:, None, None]
    return coarse_field[exposure_ids, row_block, col_block]


def draw_valid_mask(key, part):
    return stack_bits(key)[0]


def draw_images(key, part):
    shape_all = (EXPOSURES, HEIGHT, WIDTH)
    valid_mask, hit_bits = stack_bits(key)
    sky_scene = 2.0 * jax.random.truncated_normal(jax.random.fold_in(key, 103), -4.0, 4.0, (HEIGHT, WIDTH), jnp.float32)
    read_noise = 0.5 * jax.random.truncated_normal(jax.random.fold_in(key, 104), -4.0, 4.0, shape_all, jnp.float32)
    cosmic = 8.0 + 8.0 * jax.random.uniform(jax.random.fold_in(key, 105), shape_all, jnp.float32)
    bright_blobs = blob_field(key, 201, 15)
    dark_blobs = blob_field(key, 301, 8)
    outlier = jnp.where(hit_bits == 0, 6.0, 0.0) - jnp.where(hit_bits == 1, 6.0, 0.0)
    artifacts = outlier + bright_blobs - dark_blobs
    images = sky_scene[None] + read_noise + jnp.where(valid_mask == 0, cosmic, artifacts)
    return jnp.clip(images, -80.0, 80.0).astype(jnp.float32)


def set_ends(array, stream_key, least, top_value):
    place = [jax.random.randint(jax.random.fold_in(stream_key, axis), (), 0, length) for axis, length in enumerate(array.shape)]
    longest = array.shape.index(max(array.shape))
    neighbour = place[:longest] + [(place[longest] + 1) % array.shape[longest]] + place[longest + 1:]
    return array.at[tuple(place)].set(least).at[tuple(neighbour)].set(top_value)


def setup_inputs(seed: int = 0, part: int = 0) -> dict:
    arg_keys = jax.random.split(jax.random.key(seed), 6)
    own_keys = jax.random.split(jax.random.fold_in(arg_keys[5], part), 6)
    return {
        "images": draw_images(jax.random.fold_in(jax.random.fold_in(arg_keys[5], part), 71), part),
        "valid_mask": draw_valid_mask(jax.random.fold_in(jax.random.fold_in(arg_keys[5], part), 71), part),
        "basis_index": set_ends(jax.random.randint(own_keys[2], (EXPOSURES, TILES, 2), 0, BASES), jax.random.fold_in(own_keys[2], 1), 0, BASES - 1).astype(jnp.int32),
        "match_index": set_ends(jax.random.randint(own_keys[3], (EXPOSURES, TILES, 2), 0, BASES), jax.random.fold_in(own_keys[3], 1), 0, BASES - 1).astype(jnp.int32),
        "psf_bank": jnp.clip(jnp.exp(jax.random.uniform(arg_keys[4], (BASES, KERNEL * KERNEL), jnp.float32, math.log(0.05), math.log(1.0))), 0.05, 1.0),
    }


sentinel = 1.0e30


def vary_conv(padded, kernels, blend_map):
    row_count = kernels.shape[-3]
    col_count = blend_map.shape[0]
    low_acc = jnp.zeros(kernels.shape[:-2] + (col_count,), jnp.float32)
    high_acc = jnp.zeros(kernels.shape[:-2] + (col_count,), jnp.float32)
    for row_off in range(KERNEL):
        for col_off in range(KERNEL):
            window = padded[..., row_off:row_off + row_count, col_off:col_off + col_count]
            tap_at = row_off * KERNEL + col_off
            low_acc = low_acc + kernels[..., 0, tap_at][..., None] * window
            high_acc = high_acc + kernels[..., 1, tap_at][..., None] * window
    return (1.0 - blend_map) * low_acc + blend_map * high_acc


def reference(images, valid_mask, basis_index, match_index, psf_bank):
    rim_width = KERNEL // 2
    width_all = images.shape[2]
    blend_map = jnp.arange(width_all).astype(jnp.float32) / (width_all - 1)
    normed = psf_bank / jnp.sum(psf_bank, axis=1, keepdims=True)

    def warp_one(items):
        source, tile_index = items
        kernels = jnp.repeat(normed[tile_index], TILE_ROWS, axis=0)
        return vary_conv(jnp.pad(source, rim_width), kernels, blend_map)

    warped = lax.map(warp_one, (images, basis_index))
    is_valid = valid_mask == 1
    total_sum = jnp.sum(jnp.where(is_valid, warped, 0.0), axis=0)
    valid_count = jnp.sum(valid_mask, axis=0).astype(jnp.float32)
    low_three = jnp.sort(jnp.where(is_valid, warped, sentinel), axis=0)[:3]
    high_three = jnp.sort(jnp.where(is_valid, warped, -sentinel), axis=0)[-3:]
    low_sum = low_three[0] + low_three[1] + low_three[2]
    high_sum = high_three[2] + high_three[1] + high_three[0]
    coadd_image = (total_sum - low_sum - high_sum) / (valid_count - 6.0)
    coadd_padded = jnp.pad(coadd_image, rim_width)

    def match_one(tile_index):
        kernels = jnp.repeat(normed[tile_index], TILE_ROWS, axis=0)
        return vary_conv(coadd_padded, kernels, blend_map)

    matched = lax.map(match_one, match_index)
    return coadd_image, images - matched
```

```python
import functools

import jax
import jax.numpy as jnp
from jax import lax
from jax.experimental import pallas as pl
from jax.experimental.pallas import tpu as pltpu
from jax.sharding import PartitionSpec as P

TILE_ROWS = 16
KERNEL = 9
RIM = KERNEL // 2
LANES = 128
SUB = 8
SENTINEL = 1e30
MESH = pl.DeviceIdType.MESH
BF = jnp.bfloat16
F32 = jnp.float32


def split(value):
    high = value.astype(BF)
    return high, (value - high.astype(F32)).astype(BF)


def dot(left, right):
    return jnp.dot(left, right, preferred_element_type=F32)


def kernel(
    n_exp, n_strip, n_band, chunks, depth,
    images, mask, basis, match, bank,
    coadd_out, diff_out,
    pad, cpad, stage, recv, own, w_high, w_low, conv,
    local_sem, halo_send, halo_recv, stat_send, stat_recv, co_send, co_recv,
):
    count, rows, cols = images.shape
    tiles = rows // TILE_ROWS
    span = TILE_ROWS + 2 * RIM
    n_bank = bank.shape[0]
    part = max(SUB, rows // n_exp)
    owners = rows // part
    per = count // chunks
    me = lax.axis_index("exp")
    strip = lax.axis_index("strip")
    band = lax.axis_index("band")

    def there(d_strip, d_band):
        ok = jnp.bool_(True)
        if d_strip:
            ok = ok & (strip + d_strip >= 0) & (strip + d_strip < n_strip)
        if d_band:
            ok = ok & (band + d_band >= 0) & (band + d_band < n_band)
        return ok

    steps_s = (0,) if n_strip == 1 else (0, -1, 1)
    steps_b = (0,) if n_band == 1 else (0, -1, 1)
    sides = [(a, b) for a in steps_s for b in steps_b]

    def target(d_strip, d_band, exp):
        return {"exp": exp, "strip": strip + d_strip, "band": band + d_band}

    loads = [
        pltpu.make_async_copy(
            images.at[pl.ds(c * per, per)],
            pad.at[pl.ds(c * per, per), pl.ds(SUB, rows), pl.ds(LANES, cols)],
            local_sem.at[c],
        )
        for c in range(chunks)
    ]
    for load in loads:
        load.start()
    barrier = pltpu.get_barrier_semaphore()

    def each_exp(body, first=0):
        if n_exp <= 8:
            for d in range(first, n_exp):
                body(d)
        else:
            lax.fori_loop(first, n_exp, lambda d, _: (body(d), 0)[1], 0)

    for a, b in sides:
        @pl.when(there(a, b))
        def _(a=a, b=b):
            def greet(d):
                pl.semaphore_signal(
                    barrier, inc=1,
                    device_id=target(a, b, lax.rem(me + d, n_exp)), device_id_type=MESH,
                )
            each_exp(greet, 1 if (a, b) == (0, 0) else 0)
    near_s = 1 + sum(there(a, 0).astype(jnp.int32) for a in steps_s if a)
    near_b = 1 + sum(there(0, b).astype(jnp.int32) for b in steps_b if b)

    def places(a, b, height):
        src_rows = {0: (0, rows), -1: (0, height), 1: (rows - height, height)}[a]
        dst_rows = {0: SUB, -1: SUB + rows, 1: SUB - height}[a]
        src_cols = {0: (0, cols), -1: (0, LANES), 1: (cols - LANES, LANES)}[b]
        dst_cols = {0: LANES, -1: LANES + cols, 1: 0}[b]
        return src_rows, dst_rows, src_cols, dst_cols

    def rim_copy(c, at, a, b):
        src_rows, dst_rows, src_cols, dst_cols = places(a, b, depth)
        return pltpu.make_async_remote_copy(
            src_ref=images.at[pl.ds(c * per, per), pl.ds(*src_rows), pl.ds(*src_cols)],
            dst_ref=pad.at[
                pl.ds(c * per, per), pl.ds(dst_rows, src_rows[1]), pl.ds(dst_cols, src_cols[1])
            ],
            send_sem=halo_send.at[c, at],
            recv_sem=halo_recv.at[c, at],
            device_id=target(a, b, me),
            device_id_type=MESH,
        )

    rims = [(at, a, b) for at, (a, b) in enumerate(sides) if (a, b) != (0, 0)]

    for a, b in sides:
        if (a, b) == (0, 0):
            continue

        @pl.when(jnp.logical_not(there(-a, -b)))
        def _(a=a, b=b):
            src_rows, dst_rows, src_cols, dst_cols = places(a, b, SUB)
            pad[:, dst_rows:dst_rows + src_rows[1], dst_cols:dst_cols + src_cols[1]] = jnp.zeros(
                (count, src_rows[1], src_cols[1]), F32
            )
            cpad[dst_rows:dst_rows + src_rows[1], dst_cols:dst_cols + src_cols[1]] = jnp.zeros(
                (src_rows[1], src_cols[1]), F32
            )
    if n_strip == 1:
        for start in (0, SUB + rows):
            pad[:, start:start + SUB, :] = jnp.zeros((count, SUB, cols + 2 * LANES), F32)
            cpad[start:start + SUB, :] = jnp.zeros((SUB, cols + 2 * LANES), F32)
    if n_band == 1:
        for start in (0, LANES + cols):
            pad[:, :, start:start + LANES] = jnp.zeros((count, rows + 2 * SUB, LANES), F32)
            cpad[:, start:start + LANES] = jnp.zeros((rows + 2 * SUB, LANES), F32)

    pl.semaphore_wait(barrier, near_s * near_b * n_exp - 1)
    for c in range(chunks):
        for at, a, b in rims:
            @pl.when(there(a, b))
            def _(c=c, at=at, a=a, b=b):
                rim_copy(c, at, a, b).start()

    taps = KERNEL * KERNEL
    wide = 2 * LANES
    weights = bank[...]
    normed = weights / jnp.sum(weights, axis=1, keepdims=True)
    tap = lax.broadcasted_iota(jnp.int32, (taps, wide), 0)
    col = lax.broadcasted_iota(jnp.int32, (taps, wide), 1)
    tap_row = jnp.zeros((taps, wide), jnp.int32)
    for i in range(1, KERNEL):
        tap_row = tap_row + (tap >= i * KERNEL).astype(jnp.int32)
    place = (tap - tap_row * KERNEL) * span + tap_row
    spread = jnp.where(col == place, 1.0, 0.0).astype(BF)
    part_a, rest = split(normed)
    part_b = rest
    part_c = (normed - part_a.astype(F32) - part_b.astype(F32)).astype(BF)
    base = dot(part_a, spread) + dot(part_b, spread) + dot(part_c, spread)
    y_at = lax.broadcasted_iota(jnp.int32, (TILE_ROWS, wide), 0)
    for k in range(n_bank):
        line = jnp.broadcast_to(base[k:k + 1, :], (TILE_ROWS, wide))
        for bit in range(4):
            moved = pltpu.roll(line, 1 << bit, 1)
            line = jnp.where((y_at & (1 << bit)) != 0, moved, line)
        high, low = split(line)
        w_high[k] = high
        w_low[k] = low

    lane = lax.broadcasted_iota(jnp.int32, (TILE_ROWS, cols), 1)
    blend = (band * cols + lane).astype(F32) / (cols * n_band - 1)

    def shifted(field):
        total = cols + 2 * LANES
        moved = []
        for j in range(KERNEL):
            turn = (RIM - j) % total
            whole = field if turn == 0 else pltpu.roll(field, turn, 1)
            moved.append(whole[:, LANES:LANES + cols])
        pieces = []
        fill = jnp.zeros((wide - KERNEL * span, cols), F32)
        for t in range(tiles):
            at = t * TILE_ROWS
            stack = jnp.concatenate([m[at:at + span] for m in moved] + [fill], axis=0)
            pieces.append(split(stack))
        return pieces

    def stat_copy(c, who):
        return pltpu.make_async_remote_copy(
            src_ref=stage.at[pl.ds(c * per, per), pl.ds(pl.multiple_of(who * part, part), part)],
            dst_ref=recv.at[me, pl.ds(c * per, per)],
            send_sem=stat_send.at[c, who],
            recv_sem=stat_recv.at[c, me],
            device_id=target(0, 0, who),
            device_id_type=MESH,
        )

    def stat_arrival(c, who):
        return pltpu.make_async_remote_copy(
            src_ref=stage.at[pl.ds(c * per, per), pl.ds(0, part)],
            dst_ref=recv.at[who, pl.ds(c * per, per)],
            send_sem=stat_send.at[c, 0],
            recv_sem=stat_recv.at[c, who],
            device_id=target(0, 0, who),
            device_id_type=MESH,
        )

    def warp(e, _):
        pieces = shifted(pad[e, SUB - RIM:SUB + rows + RIM, :])
        for t in range(tiles):
            s_high, s_low = pieces[t]
            first, second = basis[e, t, 0], basis[e, t, 1]
            high = jnp.concatenate([w_high[first], w_high[second]], axis=0)
            low = jnp.concatenate([w_low[first], w_low[second]], axis=0)
            got = dot(high, s_high) + dot(low, s_high) + dot(high, s_low)
            value = (1.0 - blend) * got[:TILE_ROWS] + blend * got[TILE_ROWS:]
            here = pl.ds(t * TILE_ROWS, TILE_ROWS)
            stage[e, here, :] = jnp.where(mask[e, here, :] == 1, value, SENTINEL)
        return 0

    def others(body):
        def one(d):
            who = lax.rem(me + d, n_exp)
            if owners == n_exp:
                body(who)
            else:
                @pl.when(who < owners)
                def _():
                    body(who)
        each_exp(one, 1)

    for c in range(chunks):
        loads[c].wait()
        for at, a, b in rims:
            @pl.when(there(-a, -b))
            def _(c=c, at=at, a=a, b=b):
                rim_copy(c, at, a, b).wait_recv()
        lax.fori_loop(c * per, (c + 1) * per, warp, 0)
        others(lambda who, c=c: stat_copy(c, who).start())

    def insert(state, value):
        total, number, l0, l1, l2, h0, h1, h2 = state
        valid = value < 0.5 * SENTINEL
        total = total + jnp.where(valid, value, 0.0)
        number = number + jnp.where(valid, 1.0, 0.0)
        x = value
        l0, x = jnp.minimum(l0, x), jnp.maximum(l0, x)
        l1, x = jnp.minimum(l1, x), jnp.maximum(l1, x)
        l2 = jnp.minimum(l2, x)
        x = jnp.where(valid, value, -SENTINEL)
        h0, x = jnp.maximum(h0, x), jnp.minimum(h0, x)
        h1, x = jnp.maximum(h1, x), jnp.minimum(h1, x)
        h2 = jnp.maximum(h2, x)
        return total, number, l0, l1, l2, h0, h1, h2

    def co_places(a, b):
        rows_from = 0
        src_cols = {0: (0, cols), -1: (0, LANES), 1: (cols - LANES, LANES)}[b]
        dst_cols = {0: LANES, -1: LANES + cols, 1: 0}[b]
        return src_cols, dst_cols

    def co_copy(at, a, b, source, exp):
        src_cols, dst_cols = co_places(a, b)
        if a == 0:
            src_row, height = 0, part
            dst_row = pl.multiple_of(SUB + source * part, SUB)
        elif a == -1:
            src_row, height, dst_row = 0, SUB, SUB + rows
        else:
            src_row, height, dst_row = part - SUB, SUB, 0
        slot = source if a == 0 else 0
        return pltpu.make_async_remote_copy(
            src_ref=own.at[pl.ds(src_row, height), pl.ds(*src_cols)],
            dst_ref=cpad.at[pl.ds(dst_row, height), pl.ds(dst_cols, src_cols[1])],
            send_sem=co_send.at[at, exp],
            recv_sem=co_recv.at[at, slot],
            device_id=target(a, b, exp),
            device_id_type=MESH,
        )

    def sends(a):
        if a == 0:
            return jnp.bool_(True)
        return me == (0 if a == -1 else owners - 1)

    def each_send(act):
        for at, (a, b) in enumerate(sides):
            @pl.when(there(a, b) & sends(a))
            def _(at=at, a=a, b=b):
                def one(d):
                    act(co_copy(at, a, b, me, lax.rem(me + d, n_exp)))
                each_exp(one, 1 if (a, b) == (0, 0) else 0)

    def join():
        zero = jnp.zeros((part, cols), F32)
        top = jnp.full((part, cols), SENTINEL, F32)
        state = (zero, zero, top, top, top, -top, -top, -top)
        mine = pl.ds(pl.multiple_of(me * part, part), part)
        for e in range(count):
            state = insert(state, stage[e, mine, :])

        def take(d, state):
            who = lax.rem(me + d, n_exp)
            for c in range(chunks):
                stat_arrival(c, who).wait_recv()
                for e in range(c * per, (c + 1) * per):
                    state = insert(state, recv[who, e])
            return state

        state = lax.fori_loop(1, n_exp, take, state)
        total, number, l0, l1, l2, h0, h1, h2 = state
        value = (total - (l0 + l1 + l2) - (h0 + h1 + h2)) / (number - 6.0)
        own[...] = value
        cpad[pl.ds(pl.multiple_of(SUB + me * part, SUB), part), LANES:LANES + cols] = value
        each_send(lambda copy: copy.start())

    if owners == n_exp:
        join()
    else:
        pl.when(me < owners)(join)

    for at, (a, b) in enumerate(sides):
        @pl.when(there(-a, -b))
        def _(at=at, a=a, b=b):
            if a == 0:
                if b == 0:
                    others(lambda who: co_copy(at, a, b, who, me).wait_recv())
                else:
                    for who in range(owners):
                        co_copy(at, a, b, who, me).wait_recv()
            else:
                co_copy(at, a, b, 0, me).wait_recv()

    pieces = shifted(cpad[SUB - RIM:SUB + rows + RIM, :])
    high = w_high[...].reshape(n_bank * TILE_ROWS, wide)
    low = w_low[...].reshape(n_bank * TILE_ROWS, wide)
    for t in range(tiles):
        s_high, s_low = pieces[t]
        got = dot(high, s_high) + dot(low, s_high) + dot(high, s_low)
        conv[t * n_bank:(t + 1) * n_bank] = got.reshape(n_bank, TILE_ROWS, cols)
    coadd_out[...] = cpad[SUB:SUB + rows, LANES:LANES + cols]

    def final(e, _):
        for t in range(tiles):
            first, second = match[e, t, 0], match[e, t, 1]
            one, two = conv[t * n_bank + first], conv[t * n_bank + second]
            value = (1.0 - blend) * one + blend * two
            here = pl.ds(t * TILE_ROWS, TILE_ROWS)
            source = pad[e, SUB + t * TILE_ROWS:SUB + (t + 1) * TILE_ROWS, LANES:LANES + cols]
            diff_out[e, here, :] = source - value
        return 0

    lax.fori_loop(0, count, final, 0)

    for c in range(chunks):
        for at, a, b in rims:
            @pl.when(there(a, b))
            def _(c=c, at=at, a=a, b=b):
                rim_copy(c, at, a, b).wait_send()
        others(lambda who, c=c: stat_copy(c, who).wait_send())
    if owners == n_exp:
        each_send(lambda copy: copy.wait_send())
    else:
        pl.when(me < owners)(lambda: each_send(lambda copy: copy.wait_send()))


def on_device(sizes, images, valid_mask, basis_index, match_index, psf_bank):
    n_exp, n_strip, n_band = sizes
    count, rows, cols = images.shape
    chunks = 2 if count % 2 == 0 else 1
    part = max(SUB, rows // n_exp)
    owners = rows // part
    n_sides = (1 if n_strip == 1 else 3) * (1 if n_band == 1 else 3)
    tiles = rows // TILE_ROWS
    n_bank = psf_bank.shape[0]
    vmem = pl.BlockSpec(memory_space=pltpu.VMEM)
    smem = pl.BlockSpec(memory_space=pltpu.SMEM)
    dma = pltpu.SemaphoreType.DMA
    return pl.pallas_call(
        functools.partial(kernel, n_exp, n_strip, n_band, chunks, DEPTH),
        out_shape=(
            jax.ShapeDtypeStruct((rows, cols), F32),
            jax.ShapeDtypeStruct(images.shape, F32),
        ),
        in_specs=[pl.BlockSpec(memory_space=pl.ANY), vmem, smem, smem, vmem],
        out_specs=(vmem, vmem),
        scratch_shapes=[
            pltpu.VMEM((count, rows + 2 * SUB, cols + 2 * LANES), F32),
            pltpu.VMEM((rows + 2 * SUB, cols + 2 * LANES), F32),
            pltpu.VMEM((count, rows, cols), F32),
            pltpu.VMEM((n_exp, count, part, cols), F32),
            pltpu.VMEM((part, cols), F32),
            pltpu.VMEM((n_bank, TILE_ROWS, 2 * LANES), BF),
            pltpu.VMEM((n_bank, TILE_ROWS, 2 * LANES), BF),
            pltpu.VMEM((tiles * n_bank, TILE_ROWS, cols), F32),
            dma((chunks,)),
            dma((chunks, n_sides)),
            dma((chunks, n_sides)),
            dma((chunks, n_exp)),
            dma((chunks, n_exp)),
            dma((n_sides, n_exp)),
            dma((n_sides, owners)),
        ],
        compiler_params=pltpu.CompilerParams(
            collective_id=0, has_side_effects=True, vmem_limit_bytes=48 * 1024 * 1024
        ),
    )(images, valid_mask, basis_index, match_index, psf_bank)


DEPTH = RIM


def solution(mesh):
    sizes = tuple(mesh.shape[name] for name in ("exp", "strip", "band"))
    return jax.shard_map(
        functools.partial(on_device, sizes),
        mesh=mesh,
        in_specs=(
            P(("patch", "exp"), "strip", "band"),
            P(("patch", "exp"), "strip", "band"),
            P(("patch", "exp"), "strip", None),
            P(("patch", "exp"), "strip", None),
            P(),
        ),
        out_specs=(P(("patch", "strip"), "band"), P(("patch", "exp"), "strip", "band")),
        check_vma=False,
    )
```

```python
import functools

import jax
import jax.numpy as jnp
from jax import lax
from jax.experimental import pallas as pl
from jax.experimental.pallas import tpu as pltpu
from jax.sharding import PartitionSpec as P

TILE_ROWS = 16
KERNEL = 9
RIM = KERNEL // 2
LANES = 128
SUB = 8
SENTINEL = 1e30
MESH = pl.DeviceIdType.MESH
BF = jnp.bfloat16
F32 = jnp.float32


def split(value):
    high = value.astype(BF)
    return high, (value - high.astype(F32)).astype(BF)


def dot(left, right):
    return jnp.dot(left, right, preferred_element_type=F32)


def kernel(
    n_exp, n_strip, n_band, chunks, depth,
    images, mask_in, basis_in, match_in, bank_in,
    coadd_out, diff_out,
    mask, basis, match, bank,
    pad, cpad, stage, recv, own, w_high, w_low, conv,
    local_sem, in_sem, halo_send, halo_recv, stat_send, stat_recv, co_send, co_recv,
):
    count, rows, cols = images.shape
    tiles = rows // TILE_ROWS
    span = TILE_ROWS + 2 * RIM
    n_bank = bank_in.shape[0]
    part = max(SUB, rows // n_exp)
    owners = rows // part
    per = count // chunks
    me = lax.axis_index("exp")
    strip = lax.axis_index("strip")
    band = lax.axis_index("band")

    def there(d_strip, d_band):
        ok = jnp.bool_(True)
        if d_strip:
            ok = ok & (strip + d_strip >= 0) & (strip + d_strip < n_strip)
        if d_band:
            ok = ok & (band + d_band >= 0) & (band + d_band < n_band)
        return ok

    steps_s = (0,) if n_strip == 1 else (0, -1, 1)
    steps_b = (0,) if n_band == 1 else (0, -1, 1)
    sides = [(a, b) for a in steps_s for b in steps_b]

    def target(d_strip, d_band, exp):
        return {"exp": exp, "strip": strip + d_strip, "band": band + d_band}

    barrier = pltpu.get_barrier_semaphore()

    def each_exp(body, first=0):
        if n_exp <= 8:
            for d in range(first, n_exp):
                body(d)
        else:
            lax.fori_loop(first, n_exp, lambda d, _: (body(d), 0)[1], 0)

    for a, b in sides:
        @pl.when(there(a, b))
        def _(a=a, b=b):
            def greet(d):
                pl.semaphore_signal(
                    barrier, inc=1,
                    device_id=target(a, b, lax.rem(me + d, n_exp)), device_id_type=MESH,
                )
            each_exp(greet, 1 if (a, b) == (0, 0) else 0)
    loads = [
        pltpu.make_async_copy(
            images.at[pl.ds(c * per, per)],
            pad.at[pl.ds(c * per, per), pl.ds(SUB, rows), pl.ds(LANES, cols)],
            local_sem.at[c],
        )
        for c in range(chunks)
    ]
    bank_load = pltpu.make_async_copy(bank_in, bank, in_sem.at[0])
    mask_load = pltpu.make_async_copy(mask_in, mask, in_sem.at[1])
    basis_load = pltpu.make_async_copy(basis_in, basis, in_sem.at[2])
    match_load = pltpu.make_async_copy(match_in, match, in_sem.at[3])
    for load in [bank_load] + loads + [mask_load, basis_load, match_load]:
        load.start()

    near_s = 1 + sum(there(a, 0).astype(jnp.int32) for a in steps_s if a)
    near_b = 1 + sum(there(0, b).astype(jnp.int32) for b in steps_b if b)

    def places(a, b, height):
        src_rows = {0: (0, rows), -1: (0, height), 1: (rows - height, height)}[a]
        dst_rows = {0: SUB, -1: SUB + rows, 1: SUB - height}[a]
        src_cols = {0: (0, cols), -1: (0, LANES), 1: (cols - LANES, LANES)}[b]
        dst_cols = {0: LANES, -1: LANES + cols, 1: 0}[b]
        return src_rows, dst_rows, src_cols, dst_cols

    def rim_copy(c, at, a, b):
        src_rows, dst_rows, src_cols, dst_cols = places(a, b, depth)
        return pltpu.make_async_remote_copy(
            src_ref=pad.at[
                pl.ds(c * per, per),
                pl.ds(SUB + src_rows[0], src_rows[1]),
                pl.ds(LANES + src_cols[0], src_cols[1]),
            ],
            dst_ref=pad.at[
                pl.ds(c * per, per), pl.ds(dst_rows, src_rows[1]), pl.ds(dst_cols, src_cols[1])
            ],
            send_sem=halo_send.at[c, at],
            recv_sem=halo_recv.at[c, at],
            device_id=target(a, b, me),
            device_id_type=MESH,
        )

    rims = [(at, a, b) for at, (a, b) in enumerate(sides) if (a, b) != (0, 0)]

    for a, b in sides:
        if (a, b) == (0, 0):
            continue

        @pl.when(jnp.logical_not(there(-a, -b)))
        def _(a=a, b=b):
            src_rows, dst_rows, src_cols, dst_cols = places(a, b, SUB)
            pad[:, dst_rows:dst_rows + src_rows[1], dst_cols:dst_cols + src_cols[1]] = jnp.zeros(
                (count, src_rows[1], src_cols[1]), F32
            )
            cpad[dst_rows:dst_rows + src_rows[1], dst_cols:dst_cols + src_cols[1]] = jnp.zeros(
                (src_rows[1], src_cols[1]), F32
            )
    if n_strip == 1:
        for start in (0, SUB + rows):
            pad[:, start:start + SUB, :] = jnp.zeros((count, SUB, cols + 2 * LANES), F32)
            cpad[start:start + SUB, :] = jnp.zeros((SUB, cols + 2 * LANES), F32)
    if n_band == 1:
        for start in (0, LANES + cols):
            pad[:, :, start:start + LANES] = jnp.zeros((count, rows + 2 * SUB, LANES), F32)
            cpad[:, start:start + LANES] = jnp.zeros((rows + 2 * SUB, LANES), F32)

    taps = KERNEL * KERNEL
    wide = 2 * LANES
    bank_load.wait()
    weights = bank[...]
    normed = weights / jnp.sum(weights, axis=1, keepdims=True)
    tap = lax.broadcasted_iota(jnp.int32, (taps, wide), 0)
    col = lax.broadcasted_iota(jnp.int32, (taps, wide), 1)
    tap_row = jnp.zeros((taps, wide), jnp.int32)
    for i in range(1, KERNEL):
        tap_row = tap_row + (tap >= i * KERNEL).astype(jnp.int32)
    place = (tap - tap_row * KERNEL) * span + tap_row
    spread = jnp.where(col == place, 1.0, 0.0).astype(BF)
    part_a, rest = split(normed)
    part_b = rest
    part_c = (normed - part_a.astype(F32) - part_b.astype(F32)).astype(BF)
    base = dot(part_a, spread) + dot(part_b, spread) + dot(part_c, spread)
    y_at = lax.broadcasted_iota(jnp.int32, (TILE_ROWS, wide), 0)
    for k in range(n_bank):
        line = jnp.broadcast_to(base[k:k + 1, :], (TILE_ROWS, wide))
        for bit in range(4):
            moved = pltpu.roll(line, 1 << bit, 1)
            line = jnp.where((y_at & (1 << bit)) != 0, moved, line)
        high, low = split(line)
        w_high[k] = high
        w_low[k] = low

    pl.semaphore_wait(barrier, near_s * near_b * n_exp - 1)
    for c in range(chunks):
        loads[c].wait()
        for at, a, b in rims:
            @pl.when(there(a, b))
            def _(c=c, at=at, a=a, b=b):
                rim_copy(c, at, a, b).start()

    lane = lax.broadcasted_iota(jnp.int32, (TILE_ROWS, cols), 1)
    blend = (band * cols + lane).astype(F32) / (cols * n_band - 1)

    def shifted(field):
        total = cols + 2 * LANES
        moved = []
        for j in range(KERNEL):
            turn = (RIM - j) % total
            whole = field if turn == 0 else pltpu.roll(field, turn, 1)
            moved.append(whole[:, LANES:LANES + cols])
        pieces = []
        fill = jnp.zeros((wide - KERNEL * span, cols), F32)
        for t in range(tiles):
            at = t * TILE_ROWS
            stack = jnp.concatenate([m[at:at + span] for m in moved] + [fill], axis=0)
            pieces.append(split(stack))
        return pieces

    def stat_copy(c, who):
        return pltpu.make_async_remote_copy(
            src_ref=stage.at[pl.ds(c * per, per), pl.ds(pl.multiple_of(who * part, part), part)],
            dst_ref=recv.at[me, pl.ds(c * per, per)],
            send_sem=stat_send.at[c, who],
            recv_sem=stat_recv.at[c, me],
            device_id=target(0, 0, who),
            device_id_type=MESH,
        )

    def stat_arrival(c, who):
        return pltpu.make_async_remote_copy(
            src_ref=stage.at[pl.ds(c * per, per), pl.ds(0, part)],
            dst_ref=recv.at[who, pl.ds(c * per, per)],
            send_sem=stat_send.at[c, 0],
            recv_sem=stat_recv.at[c, who],
            device_id=target(0, 0, who),
            device_id_type=MESH,
        )

    def warp(e, _):
        pieces = shifted(pad[e, SUB - RIM:SUB + rows + RIM, :])
        for t in range(tiles):
            s_high, s_low = pieces[t]
            first, second = basis[t, 0, e], basis[t, 1, e]
            high = jnp.concatenate([w_high[first], w_high[second]], axis=0)
            low = jnp.concatenate([w_low[first], w_low[second]], axis=0)
            got = dot(high, s_high) + dot(low, s_high) + dot(high, s_low)
            value = (1.0 - blend) * got[:TILE_ROWS] + blend * got[TILE_ROWS:]
            here = pl.ds(t * TILE_ROWS, TILE_ROWS)
            stage[e, here, :] = jnp.where(mask[e, here, :] == 1, value, SENTINEL)
        return 0

    def others(body):
        def one(d):
            who = lax.rem(me + d, n_exp)
            if owners == n_exp:
                body(who)
            else:
                @pl.when(who < owners)
                def _():
                    body(who)
        each_exp(one, 1)

    mask_load.wait()
    basis_load.wait()
    for c in range(chunks):
        for at, a, b in rims:
            @pl.when(there(-a, -b))
            def _(c=c, at=at, a=a, b=b):
                rim_copy(c, at, a, b).wait_recv()
        lax.fori_loop(c * per, (c + 1) * per, warp, 0)
        others(lambda who, c=c: stat_copy(c, who).start())

    def insert(state, value):
        total, number, l0, l1, l2, h0, h1, h2 = state
        valid = value < 0.5 * SENTINEL
        total = total + jnp.where(valid, value, 0.0)
        number = number + jnp.where(valid, 1.0, 0.0)
        x = value
        l0, x = jnp.minimum(l0, x), jnp.maximum(l0, x)
        l1, x = jnp.minimum(l1, x), jnp.maximum(l1, x)
        l2 = jnp.minimum(l2, x)
        x = jnp.where(valid, value, -SENTINEL)
        h0, x = jnp.maximum(h0, x), jnp.minimum(h0, x)
        h1, x = jnp.maximum(h1, x), jnp.minimum(h1, x)
        h2 = jnp.maximum(h2, x)
        return total, number, l0, l1, l2, h0, h1, h2

    def co_places(a, b):
        rows_from = 0
        src_cols = {0: (0, cols), -1: (0, LANES), 1: (cols - LANES, LANES)}[b]
        dst_cols = {0: LANES, -1: LANES + cols, 1: 0}[b]
        return src_cols, dst_cols

    def co_copy(at, a, b, source, exp):
        src_cols, dst_cols = co_places(a, b)
        if a == 0:
            src_row, height = 0, part
            dst_row = pl.multiple_of(SUB + source * part, SUB)
        elif a == -1:
            src_row, height, dst_row = 0, SUB, SUB + rows
        else:
            src_row, height, dst_row = part - SUB, SUB, 0
        slot = source if a == 0 else 0
        return pltpu.make_async_remote_copy(
            src_ref=own.at[pl.ds(src_row, height), pl.ds(*src_cols)],
            dst_ref=cpad.at[pl.ds(dst_row, height), pl.ds(dst_cols, src_cols[1])],
            send_sem=co_send.at[at, exp],
            recv_sem=co_recv.at[at, slot],
            device_id=target(a, b, exp),
            device_id_type=MESH,
        )

    def sends(a):
        if a == 0:
            return jnp.bool_(True)
        return me == (0 if a == -1 else owners - 1)

    def each_send(act):
        for at, (a, b) in enumerate(sides):
            @pl.when(there(a, b) & sends(a))
            def _(at=at, a=a, b=b):
                def one(d):
                    act(co_copy(at, a, b, me, lax.rem(me + d, n_exp)))
                each_exp(one, 1 if (a, b) == (0, 0) else 0)

    def join():
        zero = jnp.zeros((part, cols), F32)
        top = jnp.full((part, cols), SENTINEL, F32)
        state = (zero, zero, top, top, top, -top, -top, -top)
        mine = pl.ds(pl.multiple_of(me * part, part), part)
        for e in range(count):
            state = insert(state, stage[e, mine, :])

        def take(d, state):
            who = lax.rem(me + d, n_exp)
            for c in range(chunks):
                stat_arrival(c, who).wait_recv()
                for e in range(c * per, (c + 1) * per):
                    state = insert(state, recv[who, e])
            return state

        state = lax.fori_loop(1, n_exp, take, state)
        total, number, l0, l1, l2, h0, h1, h2 = state
        value = (total - (l0 + l1 + l2) - (h0 + h1 + h2)) / (number - 6.0)
        own[...] = value
        cpad[pl.ds(pl.multiple_of(SUB + me * part, SUB), part), LANES:LANES + cols] = value
        each_send(lambda copy: copy.start())

    if owners == n_exp:
        join()
    else:
        pl.when(me < owners)(join)

    for at, (a, b) in enumerate(sides):
        @pl.when(there(-a, -b))
        def _(at=at, a=a, b=b):
            if a == 0:
                if b == 0:
                    others(lambda who: co_copy(at, a, b, who, me).wait_recv())
                else:
                    for who in range(owners):
                        co_copy(at, a, b, who, me).wait_recv()
            else:
                co_copy(at, a, b, 0, me).wait_recv()

    pieces = shifted(cpad[SUB - RIM:SUB + rows + RIM, :])
    high = w_high[...].reshape(n_bank * TILE_ROWS, wide)
    low = w_low[...].reshape(n_bank * TILE_ROWS, wide)
    for t in range(tiles):
        s_high, s_low = pieces[t]
        got = dot(high, s_high) + dot(low, s_high) + dot(high, s_low)
        conv[t * n_bank:(t + 1) * n_bank] = got.reshape(n_bank, TILE_ROWS, cols)
    coadd_out[...] = cpad[SUB:SUB + rows, LANES:LANES + cols]

    match_load.wait()

    def final(e, _):
        for t in range(tiles):
            first, second = match[t, 0, e], match[t, 1, e]
            one, two = conv[t * n_bank + first], conv[t * n_bank + second]
            value = (1.0 - blend) * one + blend * two
            here = pl.ds(t * TILE_ROWS, TILE_ROWS)
            source = pad[e, SUB + t * TILE_ROWS:SUB + (t + 1) * TILE_ROWS, LANES:LANES + cols]
            diff_out[e, here, :] = source - value
        return 0

    lax.fori_loop(0, count, final, 0)

    for c in range(chunks):
        for at, a, b in rims:
            @pl.when(there(a, b))
            def _(c=c, at=at, a=a, b=b):
                rim_copy(c, at, a, b).wait_send()
        others(lambda who, c=c: stat_copy(c, who).wait_send())
    if owners == n_exp:
        each_send(lambda copy: copy.wait_send())
    else:
        pl.when(me < owners)(lambda: each_send(lambda copy: copy.wait_send()))


def deliver(count, coadd, diff, coadd_out, diff_out, sem):
    half = max(count // 2, 1)
    copies = [
        pltpu.make_async_copy(coadd, coadd_out, sem.at[0]),
        pltpu.make_async_copy(diff.at[:half], diff_out.at[:half], sem.at[1]),
    ]
    if count > half:
        copies.append(pltpu.make_async_copy(diff.at[half:], diff_out.at[half:], sem.at[2]))
    for copy in copies:
        copy.start()
    for copy in copies:
        copy.wait()


def on_device(sizes, images, valid_mask, basis_index, match_index, psf_bank):
    n_exp, n_strip, n_band = sizes
    count, rows, cols = images.shape
    chunks = 2 if count % 2 == 0 else 1
    part = max(SUB, rows // n_exp)
    owners = rows // part
    n_sides = (1 if n_strip == 1 else 3) * (1 if n_band == 1 else 3)
    tiles = rows // TILE_ROWS
    n_bank = psf_bank.shape[0]
    vmem = pl.BlockSpec(memory_space=pltpu.VMEM)
    dma = pltpu.SemaphoreType.DMA
    results = pl.pallas_call(
        functools.partial(kernel, n_exp, n_strip, n_band, chunks, DEPTH),
        out_shape=(
            OUT_TYPE((rows, cols), F32),
            OUT_TYPE(images.shape, F32),
        ),
        in_specs=[pl.BlockSpec(memory_space=pltpu.HBM)] * 5,
        out_specs=(vmem, vmem),
        scratch_shapes=[
            pltpu.VMEM(valid_mask.shape, jnp.int32),
            pltpu.SMEM((tiles, 2, count), jnp.int32),
            pltpu.SMEM((tiles, 2, count), jnp.int32),
            pltpu.VMEM(psf_bank.shape, F32),
            pltpu.VMEM((count, rows + 2 * SUB, cols + 2 * LANES), F32),
            pltpu.VMEM((rows + 2 * SUB, cols + 2 * LANES), F32),
            pltpu.VMEM((count, rows, cols), F32),
            pltpu.VMEM((n_exp, count, part, cols), F32),
            pltpu.VMEM((part, cols), F32),
            pltpu.VMEM((n_bank, TILE_ROWS, 2 * LANES), BF),
            pltpu.VMEM((n_bank, TILE_ROWS, 2 * LANES), BF),
            pltpu.VMEM((tiles * n_bank, TILE_ROWS, cols), F32),
            dma((chunks,)),
            dma((4,)),
            dma((chunks, n_sides)),
            dma((chunks, n_sides)),
            dma((chunks, n_exp)),
            dma((chunks, n_exp)),
            dma((n_sides, n_exp)),
            dma((n_sides, owners)),
        ],
        compiler_params=pltpu.CompilerParams(
            collective_id=0, has_side_effects=True, vmem_limit_bytes=LIMIT
        ),
    )(
        images, valid_mask, basis_index.transpose(1, 2, 0), match_index.transpose(1, 2, 0), psf_bank
    )
    return pl.pallas_call(
        functools.partial(deliver, count),
        out_shape=(
            jax.ShapeDtypeStruct((rows, cols), F32),
            jax.ShapeDtypeStruct(images.shape, F32),
        ),
        in_specs=[IN_SPEC, IN_SPEC],
        out_specs=(pl.BlockSpec(memory_space=pltpu.HBM),) * 2,
        scratch_shapes=[dma((3,))],
        compiler_params=pltpu.CompilerParams(vmem_limit_bytes=1024 * 1024),
    )(*results)


DEPTH = RIM
LIMIT = 62 * 1024 * 1024
OUT_TYPE = pltpu.VMEM
IN_SPEC = pl.BlockSpec(memory_space=pltpu.VMEM)


def solution(mesh):
    sizes = tuple(mesh.shape[name] for name in ("exp", "strip", "band"))
    return jax.shard_map(
        functools.partial(on_device, sizes),
        mesh=mesh,
        in_specs=(
            P(("patch", "exp"), "strip", "band"),
            P(("patch", "exp"), "strip", "band"),
            P(("patch", "exp"), "strip", None),
            P(("patch", "exp"), "strip", None),
            P(),
        ),
        out_specs=(P(("patch", "strip"), "band"), P(("patch", "exp"), "strip", "band")),
        check_vma=False,
    )
```

```python
import functools

import jax
import jax.numpy as jnp
from jax import lax
from jax.experimental import pallas as pl
from jax.experimental.pallas import tpu as pltpu
from jax.sharding import PartitionSpec as P

TILE_ROWS = 16
KERNEL = 9
RIM = KERNEL // 2
LANES = 128
SUB = 8
SENTINEL = 1e30
MESH = pl.DeviceIdType.MESH
BF = jnp.bfloat16
F32 = jnp.float32


def split(value):
    high = value.astype(BF)
    return high, (value - high.astype(F32)).astype(BF)


def dot(left, right):
    return jnp.dot(left, right, preferred_element_type=F32)


def kernel(
    n_exp, n_strip, n_band, chunks, depth,
    images, mask_in, basis_in, match_in, bank_in,
    coadd_out, diff_out,
    mask, basis, match, bank,
    pad, cpad, stage, recv, own, w_high, w_low, conv,
    local_sem, in_sem, halo_send, halo_recv, stat_send, stat_recv, co_send, co_recv,
):
    count, rows, cols = images.shape
    tiles = rows // TILE_ROWS
    span = TILE_ROWS + 2 * RIM
    n_bank = bank_in.shape[0]
    part = max(SUB, rows // n_exp)
    owners = rows // part
    per = count // chunks
    me = lax.axis_index("exp")
    strip = lax.axis_index("strip")
    band = lax.axis_index("band")

    def there(d_strip, d_band):
        ok = jnp.bool_(True)
        if d_strip:
            ok = ok & (strip + d_strip >= 0) & (strip + d_strip < n_strip)
        if d_band:
            ok = ok & (band + d_band >= 0) & (band + d_band < n_band)
        return ok

    steps_s = (0,) if n_strip == 1 else (0, -1, 1)
    steps_b = (0,) if n_band == 1 else (0, -1, 1)
    sides = [(a, b) for a in steps_s for b in steps_b]

    def target(d_strip, d_band, exp):
        return {"exp": exp, "strip": strip + d_strip, "band": band + d_band}

    barrier = pltpu.get_barrier_semaphore()

    def each_exp(body, first=0):
        if n_exp <= 8:
            for d in range(n_exp - 1, first - 1, -1):
                body(d)
        else:
            lax.fori_loop(first, n_exp, lambda d, _: (body(d), 0)[1], 0)

    for a, b in sides:
        @pl.when(there(a, b))
        def _(a=a, b=b):
            def greet(d):
                pl.semaphore_signal(
                    barrier, inc=1,
                    device_id=target(a, b, lax.rem(me + d, n_exp)), device_id_type=MESH,
                )
            each_exp(greet, 1 if (a, b) == (0, 0) else 0)
    loads = [
        pltpu.make_async_copy(
            images.at[pl.ds(c * per, per)],
            pad.at[pl.ds(c * per, per), pl.ds(SUB, rows), pl.ds(LANES, cols)],
            local_sem.at[c],
        )
        for c in range(chunks)
    ]
    bank_load = pltpu.make_async_copy(bank_in, bank, in_sem.at[0])
    mask_load = pltpu.make_async_copy(mask_in, mask, in_sem.at[1])
    basis_load = pltpu.make_async_copy(basis_in, basis, in_sem.at[2])
    match_load = pltpu.make_async_copy(match_in, match, in_sem.at[3])
    for load in [bank_load] + loads + [mask_load, basis_load, match_load]:
        load.start()

    near_s = 1 + sum(there(a, 0).astype(jnp.int32) for a in steps_s if a)
    near_b = 1 + sum(there(0, b).astype(jnp.int32) for b in steps_b if b)

    def places(a, b, height):
        src_rows = {0: (0, rows), -1: (0, height), 1: (rows - height, height)}[a]
        dst_rows = {0: SUB, -1: SUB + rows, 1: SUB - height}[a]
        src_cols = {0: (0, cols), -1: (0, LANES), 1: (cols - LANES, LANES)}[b]
        dst_cols = {0: LANES, -1: LANES + cols, 1: 0}[b]
        return src_rows, dst_rows, src_cols, dst_cols

    def rim_copy(c, at, a, b):
        src_rows, dst_rows, src_cols, dst_cols = places(a, b, depth)
        return pltpu.make_async_remote_copy(
            src_ref=pad.at[
                pl.ds(c * per, per),
                pl.ds(SUB + src_rows[0], src_rows[1]),
                pl.ds(LANES + src_cols[0], src_cols[1]),
            ],
            dst_ref=pad.at[
                pl.ds(c * per, per), pl.ds(dst_rows, src_rows[1]), pl.ds(dst_cols, src_cols[1])
            ],
            send_sem=halo_send.at[c, at],
            recv_sem=halo_recv.at[c, at],
            device_id=target(a, b, me),
            device_id_type=MESH,
        )

    rims = [(at, a, b) for at, (a, b) in enumerate(sides) if (a, b) != (0, 0)]

    for a, b in sides:
        if (a, b) == (0, 0):
            continue

        @pl.when(jnp.logical_not(there(-a, -b)))
        def _(a=a, b=b):
            src_rows, dst_rows, src_cols, dst_cols = places(a, b, SUB)
            pad[:, dst_rows:dst_rows + src_rows[1], dst_cols:dst_cols + src_cols[1]] = jnp.zeros(
                (count, src_rows[1], src_cols[1]), F32
            )
            cpad[dst_rows:dst_rows + src_rows[1], dst_cols:dst_cols + src_cols[1]] = jnp.zeros(
                (src_rows[1], src_cols[1]), F32
            )
    if n_strip == 1:
        for start in (0, SUB + rows):
            pad[:, start:start + SUB, :] = jnp.zeros((count, SUB, cols + 2 * LANES), F32)
            cpad[start:start + SUB, :] = jnp.zeros((SUB, cols + 2 * LANES), F32)
    if n_band == 1:
        for start in (0, LANES + cols):
            pad[:, :, start:start + LANES] = jnp.zeros((count, rows + 2 * SUB, LANES), F32)
            cpad[:, start:start + LANES] = jnp.zeros((rows + 2 * SUB, LANES), F32)

    taps = KERNEL * KERNEL
    wide = 2 * LANES
    bank_load.wait()
    weights = bank[...]
    normed = weights / jnp.sum(weights, axis=1, keepdims=True)
    tap = lax.broadcasted_iota(jnp.int32, (taps, wide), 0)
    col = lax.broadcasted_iota(jnp.int32, (taps, wide), 1)
    tap_row = jnp.zeros((taps, wide), jnp.int32)
    for i in range(1, KERNEL):
        tap_row = tap_row + (tap >= i * KERNEL).astype(jnp.int32)
    place = (tap - tap_row * KERNEL) * span + tap_row
    spread = jnp.where(col == place, 1.0, 0.0).astype(BF)
    part_a, rest = split(normed)
    part_b = rest
    part_c = (normed - part_a.astype(F32) - part_b.astype(F32)).astype(BF)
    base = dot(part_a, spread) + dot(part_b, spread) + dot(part_c, spread)
    y_at = lax.broadcasted_iota(jnp.int32, (TILE_ROWS, wide), 0)
    for k in range(n_bank):
        line = jnp.broadcast_to(base[k:k + 1, :], (TILE_ROWS, wide))
        for bit in range(4):
            moved = pltpu.roll(line, 1 << bit, 1)
            line = jnp.where((y_at & (1 << bit)) != 0, moved, line)
        high, low = split(line)
        w_high[k] = high
        w_low[k] = low

    pl.semaphore_wait(barrier, near_s * near_b * n_exp - 1)
    for c in range(chunks):
        loads[c].wait()
        for at, a, b in rims:
            @pl.when(there(a, b))
            def _(c=c, at=at, a=a, b=b):
                rim_copy(c, at, a, b).start()

    lane = lax.broadcasted_iota(jnp.int32, (TILE_ROWS, cols), 1)
    blend = (band * cols + lane).astype(F32) / (cols * n_band - 1)

    def shifted(field):
        total = cols + 2 * LANES
        moved = []
        for j in range(KERNEL):
            turn = (RIM - j) % total
            whole = field if turn == 0 else pltpu.roll(field, turn, 1)
            moved.append(whole[:, LANES:LANES + cols])
        pieces = []
        fill = jnp.zeros((wide - KERNEL * span, cols), F32)
        for t in range(tiles):
            at = t * TILE_ROWS
            stack = jnp.concatenate([m[at:at + span] for m in moved] + [fill], axis=0)
            pieces.append(split(stack))
        return pieces

    def stat_copy(c, who):
        return pltpu.make_async_remote_copy(
            src_ref=stage.at[pl.ds(c * per, per), pl.ds(pl.multiple_of(who * part, part), part)],
            dst_ref=recv.at[me, pl.ds(c * per, per)],
            send_sem=stat_send.at[c, who],
            recv_sem=stat_recv.at[c, me],
            device_id=target(0, 0, who),
            device_id_type=MESH,
        )

    def stat_arrival(c, who):
        return pltpu.make_async_remote_copy(
            src_ref=stage.at[pl.ds(c * per, per), pl.ds(0, part)],
            dst_ref=recv.at[who, pl.ds(c * per, per)],
            send_sem=stat_send.at[c, 0],
            recv_sem=stat_recv.at[c, who],
            device_id=target(0, 0, who),
            device_id_type=MESH,
        )

    def warp(e, _):
        pieces = shifted(pad[e, SUB - RIM:SUB + rows + RIM, :])
        for t in range(tiles):
            s_high, s_low = pieces[t]
            first, second = basis[t, 0, e], basis[t, 1, e]
            high = jnp.concatenate([w_high[first], w_high[second]], axis=0)
            low = jnp.concatenate([w_low[first], w_low[second]], axis=0)
            both = dot(jnp.concatenate([high, low], axis=0), s_high)
            got = both[:2 * TILE_ROWS] + both[2 * TILE_ROWS:] + dot(high, s_low)
            value = (1.0 - blend) * got[:TILE_ROWS] + blend * got[TILE_ROWS:]
            here = pl.ds(t * TILE_ROWS, TILE_ROWS)
            stage[e, here, :] = jnp.where(mask[e, here, :] == 1, value, SENTINEL)
        return 0

    def others(body):
        def one(d):
            who = lax.rem(me + d, n_exp)
            if owners == n_exp:
                body(who)
            else:
                @pl.when(who < owners)
                def _():
                    body(who)
        each_exp(one, 1)

    mask_load.wait()
    basis_load.wait()
    for c in range(chunks):
        for at, a, b in rims:
            @pl.when(there(-a, -b))
            def _(c=c, at=at, a=a, b=b):
                rim_copy(c, at, a, b).wait_recv()
        lax.fori_loop(c * per, (c + 1) * per, warp, 0, unroll=True)
        others(lambda who, c=c: stat_copy(c, who).start())

    def insert(state, value):
        total, number, l0, l1, l2, h0, h1, h2 = state
        valid = value < 0.5 * SENTINEL
        total = total + jnp.where(valid, value, 0.0)
        number = number + jnp.where(valid, 1.0, 0.0)
        x = value
        l0, x = jnp.minimum(l0, x), jnp.maximum(l0, x)
        l1, x = jnp.minimum(l1, x), jnp.maximum(l1, x)
        l2 = jnp.minimum(l2, x)
        x = jnp.where(valid, value, -SENTINEL)
        h0, x = jnp.maximum(h0, x), jnp.minimum(h0, x)
        h1, x = jnp.maximum(h1, x), jnp.minimum(h1, x)
        h2 = jnp.maximum(h2, x)
        return total, number, l0, l1, l2, h0, h1, h2

    def co_places(a, b):
        rows_from = 0
        src_cols = {0: (0, cols), -1: (0, LANES), 1: (cols - LANES, LANES)}[b]
        dst_cols = {0: LANES, -1: LANES + cols, 1: 0}[b]
        return src_cols, dst_cols

    def co_copy(at, a, b, source, exp):
        src_cols, dst_cols = co_places(a, b)
        if a == 0:
            src_row, height = 0, part
            dst_row = pl.multiple_of(SUB + source * part, SUB)
        elif a == -1:
            src_row, height, dst_row = 0, SUB, SUB + rows
        else:
            src_row, height, dst_row = part - SUB, SUB, 0
        slot = source if a == 0 else 0
        return pltpu.make_async_remote_copy(
            src_ref=own.at[pl.ds(src_row, height), pl.ds(*src_cols)],
            dst_ref=cpad.at[pl.ds(dst_row, height), pl.ds(dst_cols, src_cols[1])],
            send_sem=co_send.at[at, exp],
            recv_sem=co_recv.at[at, slot],
            device_id=target(a, b, exp),
            device_id_type=MESH,
        )

    def sends(a):
        if a == 0:
            return jnp.bool_(True)
        return me == (0 if a == -1 else owners - 1)

    def each_send(act):
        for at, (a, b) in enumerate(sides):
            @pl.when(there(a, b) & sends(a))
            def _(at=at, a=a, b=b):
                def one(d):
                    act(co_copy(at, a, b, me, lax.rem(me + d, n_exp)))
                each_exp(one, 1 if (a, b) == (0, 0) else 0)

    def join():
        zero = jnp.zeros((part, cols), F32)
        top = jnp.full((part, cols), SENTINEL, F32)
        state = (zero, zero, top, top, top, -top, -top, -top)
        mine = pl.ds(pl.multiple_of(me * part, part), part)
        for e in range(count):
            state = insert(state, stage[e, mine, :])

        def take(d, state):
            who = lax.rem(me + d, n_exp)
            for c in range(chunks):
                stat_arrival(c, who).wait_recv()
                for e in range(c * per, (c + 1) * per):
                    state = insert(state, recv[who, e])
            return state

        state = lax.fori_loop(1, n_exp, take, state, unroll=n_exp <= 8)
        total, number, l0, l1, l2, h0, h1, h2 = state
        value = (total - (l0 + l1 + l2) - (h0 + h1 + h2)) / (number - 6.0)
        own[...] = value
        cpad[pl.ds(pl.multiple_of(SUB + me * part, SUB), part), LANES:LANES + cols] = value
        each_send(lambda copy: copy.start())

    if owners == n_exp:
        join()
    else:
        pl.when(me < owners)(join)

    for at, (a, b) in enumerate(sides):
        @pl.when(there(-a, -b))
        def _(at=at, a=a, b=b):
            if a == 0:
                if b == 0:
                    others(lambda who: co_copy(at, a, b, who, me).wait_recv())
                else:
                    for who in range(owners):
                        co_copy(at, a, b, who, me).wait_recv()
            else:
                co_copy(at, a, b, 0, me).wait_recv()

    pieces = shifted(cpad[SUB - RIM:SUB + rows + RIM, :])
    high = w_high[...].reshape(n_bank * TILE_ROWS, wide)
    low = w_low[...].reshape(n_bank * TILE_ROWS, wide)
    for t in range(tiles):
        s_high, s_low = pieces[t]
        both = dot(jnp.concatenate([high, low], axis=0), s_high)
        size = n_bank * TILE_ROWS
        got = both[:size] + both[size:] + dot(high, s_low)
        conv[t * n_bank:(t + 1) * n_bank] = got.reshape(n_bank, TILE_ROWS, cols)
    coadd_out[...] = cpad[SUB:SUB + rows, LANES:LANES + cols]

    match_load.wait()

    def final(e, _):
        for t in range(tiles):
            first, second = match[t, 0, e], match[t, 1, e]
            one, two = conv[t * n_bank + first], conv[t * n_bank + second]
            value = (1.0 - blend) * one + blend * two
            here = pl.ds(t * TILE_ROWS, TILE_ROWS)
            source = pad[e, SUB + t * TILE_ROWS:SUB + (t + 1) * TILE_ROWS, LANES:LANES + cols]
            diff_out[e, here, :] = source - value
        return 0

    lax.fori_loop(0, count, final, 0, unroll=True)

    for c in range(chunks):
        for at, a, b in rims:
            @pl.when(there(a, b))
            def _(c=c, at=at, a=a, b=b):
                rim_copy(c, at, a, b).wait_send()
        others(lambda who, c=c: stat_copy(c, who).wait_send())
    if owners == n_exp:
        each_send(lambda copy: copy.wait_send())
    else:
        pl.when(me < owners)(lambda: each_send(lambda copy: copy.wait_send()))


def deliver(count, coadd, diff, coadd_out, diff_out, sem):
    half = max(count // 2, 1)
    copies = [
        pltpu.make_async_copy(coadd, coadd_out, sem.at[0]),
        pltpu.make_async_copy(diff.at[:half], diff_out.at[:half], sem.at[1]),
    ]
    if count > half:
        copies.append(pltpu.make_async_copy(diff.at[half:], diff_out.at[half:], sem.at[2]))
    for copy in copies:
        copy.start()
    for copy in copies:
        copy.wait()


def on_device(sizes, images, valid_mask, basis_index, match_index, psf_bank):
    n_exp, n_strip, n_band = sizes
    count, rows, cols = images.shape
    chunks = 2 if count % 2 == 0 else 1
    part = max(SUB, rows // n_exp)
    owners = rows // part
    n_sides = (1 if n_strip == 1 else 3) * (1 if n_band == 1 else 3)
    tiles = rows // TILE_ROWS
    n_bank = psf_bank.shape[0]
    vmem = pl.BlockSpec(memory_space=pltpu.VMEM)
    dma = pltpu.SemaphoreType.DMA
    results = pl.pallas_call(
        functools.partial(kernel, n_exp, n_strip, n_band, chunks, DEPTH),
        out_shape=(
            OUT_TYPE((rows, cols), F32),
            OUT_TYPE(images.shape, F32),
        ),
        in_specs=[pl.BlockSpec(memory_space=pltpu.HBM)] * 5,
        out_specs=(vmem, vmem),
        scratch_shapes=[
            pltpu.VMEM(valid_mask.shape, jnp.int32),
            pltpu.SMEM((tiles, 2, count), jnp.int32),
            pltpu.SMEM((tiles, 2, count), jnp.int32),
            pltpu.VMEM(psf_bank.shape, F32),
            pltpu.VMEM((count, rows + 2 * SUB, cols + 2 * LANES), F32),
            pltpu.VMEM((rows + 2 * SUB, cols + 2 * LANES), F32),
            pltpu.VMEM((count, rows, cols), F32),
            pltpu.VMEM((n_exp, count, part, cols), F32),
            pltpu.VMEM((part, cols), F32),
            pltpu.VMEM((n_bank, TILE_ROWS, 2 * LANES), BF),
            pltpu.VMEM((n_bank, TILE_ROWS, 2 * LANES), BF),
            pltpu.VMEM((tiles * n_bank, TILE_ROWS, cols), F32),
            dma((chunks,)),
            dma((4,)),
            dma((chunks, n_sides)),
            dma((chunks, n_sides)),
            dma((chunks, n_exp)),
            dma((chunks, n_exp)),
            dma((n_sides, n_exp)),
            dma((n_sides, owners)),
        ],
        compiler_params=pltpu.CompilerParams(
            collective_id=0, has_side_effects=True, vmem_limit_bytes=LIMIT
        ),
    )(
        images, valid_mask, basis_index.transpose(1, 2, 0), match_index.transpose(1, 2, 0), psf_bank
    )
    return pl.pallas_call(
        functools.partial(deliver, count),
        out_shape=(
            jax.ShapeDtypeStruct((rows, cols), F32),
            jax.ShapeDtypeStruct(images.shape, F32),
        ),
        in_specs=[IN_SPEC, IN_SPEC],
        out_specs=(pl.BlockSpec(memory_space=pltpu.HBM),) * 2,
        scratch_shapes=[dma((3,))],
        compiler_params=pltpu.CompilerParams(vmem_limit_bytes=1024 * 1024),
    )(*results)


DEPTH = RIM
LIMIT = 62 * 1024 * 1024
OUT_TYPE = pltpu.VMEM
IN_SPEC = pl.BlockSpec(memory_space=pltpu.VMEM)


def solution(mesh):
    sizes = tuple(mesh.shape[name] for name in ("exp", "strip", "band"))
    return jax.shard_map(
        functools.partial(on_device, sizes),
        mesh=mesh,
        in_specs=(
            P(("patch", "exp"), "strip", "band"),
            P(("patch", "exp"), "strip", "band"),
            P(("patch", "exp"), "strip", None),
            P(("patch", "exp"), "strip", None),
            P(),
        ),
        out_specs=(P(("patch", "strip"), "band"), P(("patch", "exp"), "strip", "band")),
        check_vma=False,
    )
```
